32 devices in a mesh: tile: 8 (over z, y), slab: 4 (over x, core).
Axes of the slice: x: 2, y: 2, z: 4, core: 2. Of those that a mesh axis runs over, the one named last changes fastest.
Arguments:
- amplitudes: float32 [8, 768, 96], P('tile'), may hold values from -6 to 6
- cholesky: float32 [128, 768, 96], P('slab'), may hold values from -0.1820594 to 0.1820594
- pair_occ: int32 [8, 2], replicated, may hold values from 0 to 63
- hole_integrals: float32 [8, 8], replicated, may hold values from -6 to 6
- other_terms: float32 [8, 768, 96], P('tile', 'slab'), may hold values from -6 to 6
- occ_energy: float32 [64], replicated, may hold values from -2 to -0.4
- vir_energy: float32 [768], replicated, may hold values from 0.2 to 3
Outputs:
- amp_new: float32 [8, 768, 96], P('tile', 'slab')
The draws below stay inside these ranges and needn't reach their ends.
All inputs are finite; a program needn't handle non-finite values.
Results may differ from the reference program's by a relative error of at most 0.0001.
Values sent between devices are 32-bit elements; how exact they have to be, the bound alone decides.
A program may use at most 64 MiB of HBM per device.

```python
import jax
import jax.numpy as jnp
from jax import lax

O = 64
NV = 768
OB = 8
VB = 96
PAIRS = 8
NQ = 128


def plant(array, key, smallest, largest):
    place = [jax.random.randint(jax.random.fold_in(key, axis), (), 0, length) for axis, length in enumerate(array.shape)]
    main_axis = array.shape.index(max(array.shape))
    next_to = place[:main_axis] + [(place[main_axis] + 1) % array.shape[main_axis]] + place[main_axis + 1:]
    return array.at[tuple(place)].set(smallest).at[tuple(next_to)].set(largest)


def levels(stream_key, extent, shards, smallest, top_value):
    gain, own = 1.0, jax.random.fold_in(stream_key, 6)
    for dim, parts in shards:
        steps = jnp.exp(jax.random.uniform(jax.random.fold_in(own, dim), (parts,), jnp.float32, smallest / len(shards), top_value / len(shards)))
        gain = gain * jnp.repeat(steps, extent[dim] // parts).reshape([-1 if axis == dim else 1 for axis in range(len(extent))])
    return gain


def gaussian(stream_key, extent, scale, most, cuts=(), kind=jnp.bfloat16):
    entries = jax.random.normal(stream_key, extent, jnp.float32) * scale
    if len(cuts) > 0:
        entries = levels(stream_key, extent, cuts, -0.22, 0.18) * entries
    return jnp.clip(entries, min=-most, max=most).astype(kind)


def setup_inputs(seed: int = 0) -> dict:
    key_list = jax.random.split(jax.random.key(seed), 8)
    amplitudes = gaussian(key_list[0], (PAIRS, NV, VB), 1.0, 6.0, ((0, 8),), jnp.float32)
    cholesky = gaussian(key_list[1], (NQ, NV, VB), ((NQ * VB * VB) ** -0.25), 0.1820594, ((0, 4),), jnp.float32)
    pair_occ = plant(jax.random.randint(key_list[2], (PAIRS, 2), 0, O), jax.random.fold_in(key_list[2], 1), 0, O - 1).astype(jnp.int32)
    hole_integrals = gaussian(key_list[3], (PAIRS, PAIRS), (PAIRS // 8) ** -0.5, 6.0, (), jnp.float32)
    other_terms = gaussian(key_list[4], (PAIRS, NV, VB), 1.0, 6.0, ((0, 8), (1, 4)), jnp.float32)
    occ_energy = jnp.clip(jax.random.uniform(key_list[5], (O,), jnp.float32, -2.0, -0.4), -2.0, -0.4)
    vir_energy = jnp.clip(jax.random.uniform(key_list[6], (NV,), jnp.float32, 0.2, 3.0), 0.2, 3.0)
    return dict(amplitudes=amplitudes, cholesky=cholesky, pair_occ=pair_occ, hole_integrals=hole_integrals, other_terms=other_terms, occ_energy=occ_energy, vir_energy=vir_energy)


def reference(amplitudes, cholesky, pair_occ, hole_integrals, other_terms, occ_energy, vir_energy):
    pairs = amplitudes.shape[0]
    irreps = jnp.bitwise_xor(pair_occ[:, 0] // OB, pair_occ[:, 1] // OB).astype(jnp.int32)
    blocks = jnp.arange(8, dtype=jnp.int32)
    partner = jnp.bitwise_xor(blocks[None, :], irreps[:, None]).astype(jnp.int32)
    tiles = amplitudes.reshape(pairs, 8, VB, VB)

    def ladder_step(total, vectors):
        left = vectors.reshape(8, VB, VB)
        right = jnp.take(left, partner, axis=0)
        middle = jnp.einsum("pkcd,pkbd->pkcb", tiles, right, precision=lax.Precision.HIGHEST)
        return total + jnp.einsum("kac,pkcb->pkab", left, middle, precision=lax.Precision.HIGHEST), None

    ladder, _ = lax.scan(ladder_step, jnp.zeros((pairs, 8, VB, VB), jnp.float32), cholesky)
    ladder = ladder.reshape(pairs, NV, VB)
    masked = hole_integrals * (irreps[:, None] == irreps[None, :]).astype(jnp.float32)
    hole = jnp.dot(masked, amplitudes.reshape(pairs, NV * VB), precision=lax.Precision.HIGHEST).reshape(pairs, NV, VB)
    residual = other_terms + ladder + hole
    pair_energy = jnp.take(occ_energy, pair_occ[:, 0]) + jnp.take(occ_energy, pair_occ[:, 1])
    partner_energy = jnp.take(vir_energy.reshape(8, VB), partner, axis=0)
    row_block = (jnp.arange(NV, dtype=jnp.int32) // VB).astype(jnp.int32)
    column_energy = jnp.take(partner_energy, row_block, axis=1)
    denominator = pair_energy[:, None, None] - vir_energy[None, :, None] - column_energy
    return residual / denominator
```

```python
import functools

import jax
import jax.numpy as jnp
from jax import lax
from jax.experimental import pallas as pl
from jax.experimental.pallas import tpu as pltpu
from jax.sharding import PartitionSpec as P

MESH = pl.DeviceIdType.MESH
BLOCKS = 8
GROUP = 8
LANES = 128


def split(x):
    hi = x.astype(jnp.bfloat16)
    lo = (x - hi.astype(jnp.float32)).astype(jnp.bfloat16)
    return hi, lo


def widen(x):
    pad = LANES - x.shape[1]
    return jnp.concatenate([x, jnp.zeros((x.shape[0], pad), x.dtype)], axis=1) if pad else x


def turned(x):
    pad = LANES - x.shape[0]
    x = jnp.concatenate([x, jnp.zeros((pad, x.shape[1]), x.dtype)], axis=0) if pad else x
    return x.T


def kernel(
    tile_n, slab_n, width, vectors, chunk, workers, occ_block,
    amp_hbm, chol_hbm, other_hbm, pair_ref, holes_ref, occ_ref, vir_ref,
    out_ref,
    amp_t, amp, chol, other, left, right, stacks, partial, landed, gathered, products, hole, energy,
    load_sem, amp_sem, other_sem, own_sem, send1, recv1, send2, recv2, send3, recv3,
):
    t = lax.axis_index("tile")
    s = lax.axis_index("slab")
    rows_dev = other.shape[0]
    piece = min(rows_dev, width)
    per_dest = rows_dev // piece
    dests_in_block = width // piece
    groups = vectors // GROUP
    row_start = s * rows_dev

    barrier = pltpu.get_barrier_semaphore()

    @pl.loop(1, tile_n)
    def _(k):
        pl.semaphore_signal(barrier, inc=1, device_id={"tile": lax.rem(t + k, tile_n)}, device_id_type=MESH)

    @pl.loop(1, slab_n)
    def _(k):
        pl.semaphore_signal(barrier, inc=1, device_id={"slab": lax.rem(s + k, slab_n)}, device_id_type=MESH)

    amp_copy = pltpu.make_async_copy(amp_hbm.at[0], amp_t, amp_sem)
    amp_copy.start()

    def load(g):
        return pltpu.make_async_copy(chol_hbm.at[pl.ds(g * GROUP, GROUP)], chol.at[g], load_sem.at[g])

    for g in range(groups):
        load(g).start()
    other_copy = pltpu.make_async_copy(other_hbm.at[0], other, other_sem)
    other_copy.start()

    amp_copy.wait()
    amp[...] = turned(amp_t[...])[:, :width]
    pl.semaphore_wait(barrier, tile_n + slab_n - 2)

    def to_worker(w):
        return pltpu.make_async_remote_copy(
            src_ref=amp.at[pl.ds(pl.multiple_of(row_start + w * chunk, 8), chunk), :],
            dst_ref=gathered.at[t],
            send_sem=send1.at[w],
            recv_sem=recv1.at[t],
            device_id={"tile": w},
            device_id_type=MESH,
        )

    @pl.loop(0, workers)
    def _(w):
        @pl.when(w != t)
        def _():
            to_worker(w).start()

    def own_chunk():
        return pltpu.make_async_copy(
            amp.at[pl.ds(pl.multiple_of(row_start + t * chunk, 8), chunk), :], gathered.at[t], own_sem
        )

    @pl.when(t < workers)
    def _():
        own_chunk().start()

    for block in range(BLOCKS):
        t_hi, t_lo = split(widen(amp[block * width : (block + 1) * width, :]))
        rows = jnp.concatenate([t_hi, t_lo], axis=1)
        zero = jnp.zeros((LANES - width, 2 * LANES), jnp.bfloat16)
        stacks[block] = jnp.concatenate([rows, zero, rows, zero], axis=0)

    def first_group(g):
        load(g).wait()
        for j in range(GROUP):
            hi, lo = split(turned(chol[g, j]))
            lanes = slice(j * LANES, (j + 1) * LANES)
            for block in range(BLOCKS):
                part = slice(block * width, (block + 1) * width)
                right[block * groups + g, :width, lanes] = hi[part]
                right[block * groups + g, width:, lanes] = lo[part]

        @pl.loop(0, BLOCKS)
        def _(block):
            at = block * groups + g
            vectors_here = [
                jnp.concatenate([right[at, :width, lanes], right[at, width:, lanes]], axis=1)
                for lanes in [slice(j * LANES, (j + 1) * LANES) for j in range(GROUP)]
            ]
            both = jnp.dot(
                jnp.concatenate(vectors_here, axis=0), stacks[block], preferred_element_type=jnp.float32
            )
            w_hi, w_lo = split(both[:, :LANES] + both[:, LANES:])
            for j in range(GROUP):
                lanes = slice(j * LANES, (j + 1) * LANES)
                part = slice(j * width, (j + 1) * width)
                left[at, :width, lanes] = w_hi[part]
                left[at, width:, lanes] = w_lo[part]

    pl.loop(0, groups)(first_group)

    def irrep(p):
        return (pair_ref[0, p] // occ_block) ^ (pair_ref[1, p] // occ_block)

    def to_pair(p):
        return pltpu.make_async_remote_copy(
            src_ref=products.at[p],
            dst_ref=hole.at[t],
            send_sem=send2.at[p],
            recv_sem=recv2.at[t],
            device_id={"tile": p},
            device_id_type=MESH,
        )

    @pl.when(t < workers)
    def _():
        own_chunk().wait()

        @pl.loop(0, tile_n)
        def _(q):
            @pl.when(q != t)
            def _():
                pltpu.make_async_remote_copy(
                    src_ref=gathered.at[q], dst_ref=gathered.at[q], send_sem=send1.at[0],
                    recv_sem=recv1.at[q], device_id={"tile": q}, device_id_type=MESH,
                ).wait_recv()

        @pl.loop(0, tile_n)
        def _(p):
            mine = irrep(p)

            def add(q, total):
                factor = jnp.where(irrep(q) == mine, holes_ref[p, q], 0.0)
                return total + factor * gathered[q]

            products[p] = lax.fori_loop(0, tile_n, add, jnp.zeros((chunk, width), jnp.float32), unroll=8)

            @pl.when(p != t)
            def _():
                to_pair(p).start()

            @pl.when(p == t)
            def _():
                hole[t] = products[p]

    s_p = irrep(t)
    chips = slab_n // 2
    x_pos, core = s // 2, lax.rem(s, 2)

    def place(k):
        if dests_in_block > 1:
            block = lax.rem(s // dests_in_block + BLOCKS - 1 - k, BLOCKS)
            return block, block * dests_in_block, 0
        d, j = k // per_dest, lax.rem(k, per_dest)
        chip = lax.rem(x_pos + chips - 1 - d // 2, chips)
        flip = lax.rem(d + chips_last(d), 2)
        dest = chip * 2 + lax.rem(core + flip, 2)
        return dest * per_dest + j, dest, j

    def chips_last(d):
        return jnp.where(d // 2 == chips - 1, 1, 0)

    def to_owner(block, dest, i, j):
        return pltpu.make_async_remote_copy(
            src_ref=partial.at[block, pl.ds(i * piece, piece), :],
            dst_ref=landed.at[s, j],
            send_sem=send3.at[dest, j],
            recv_sem=recv3.at[s, j],
            device_id={"slab": dest},
            device_id_type=MESH,
        )

    @pl.loop(0, BLOCKS)
    def _(k):
        block, dest0, j = place(k)
        partner = block ^ s_p
        total = jnp.zeros((2 * width, 2 * width), jnp.float32)
        for g in range(groups):
            total += lax.dot_general(
                left[block * groups + g], right[partner * groups + g],
                (((1,), (1,)), ((), ())), preferred_element_type=jnp.float32,
            )
        half = total[:width] + total[width:]
        partial[block] = half[:, :width] + half[:, width:]
        for i in range(dests_in_block):
            @pl.when(dest0 + i != s)
            def _():
                to_owner(block, dest0 + i, i, j).start()

    for block in range(BLOCKS):
        energy[block : block + 1, :] = vir_ref[:, block * width : (block + 1) * width]
    pair_energy = occ_ref[pair_ref[0, t]] + occ_ref[pair_ref[1, t]]
    other_copy.wait()

    @pl.loop(0, workers)
    def _(w):
        @pl.when(w != t)
        def _():
            pltpu.make_async_remote_copy(
                src_ref=hole.at[w], dst_ref=hole.at[w], send_sem=send2.at[0],
                recv_sem=recv2.at[w], device_id={"tile": w}, device_id_type=MESH,
            ).wait_recv()

    for j in range(per_dest):
        start = row_start + j * piece
        block = start // width
        offset = lax.rem(start, width)
        row_i = lax.broadcasted_iota(jnp.int32, (piece, width), 0) + offset
        col_i = lax.broadcasted_iota(jnp.int32, (piece, width), 1)
        mine = energy[pl.ds(block, 1), :]
        row_energy = jnp.sum(jnp.where(row_i == col_i, mine, 0.0), axis=1, keepdims=True)
        denominator = pair_energy - row_energy - energy[pl.ds(block ^ s_p, 1), :]
        total = partial[block, pl.ds(pl.multiple_of(offset, 8), piece), :]
        for k in range(1, slab_n):
            source = lax.rem(s + k, slab_n)
            pltpu.make_async_remote_copy(
                src_ref=landed.at[source, j], dst_ref=landed.at[source, j], send_sem=send3.at[0, 0],
                recv_sem=recv3.at[source, j], device_id={"slab": source}, device_id_type=MESH,
            ).wait_recv()
            total += landed[source, j]
        count = piece // chunk
        holes = hole[j * count : (j + 1) * count].reshape(piece, width)
        out_ref[0, j * piece : (j + 1) * piece, :] = (
            other[j * piece : (j + 1) * piece, :] + total + holes
        ) / denominator

    @pl.loop(0, workers)
    def _(w):
        @pl.when(w != t)
        def _():
            to_worker(w).wait_send()

    @pl.when(t < workers)
    def _():
        @pl.loop(0, tile_n)
        def _(p):
            @pl.when(p != t)
            def _():
                to_pair(p).wait_send()

    @pl.loop(0, BLOCKS)
    def _(k):
        block, dest0, j = place(k)
        for i in range(dests_in_block):
            @pl.when(dest0 + i != s)
            def _():
                to_owner(block, dest0 + i, i, j).wait_send()


def local(amplitudes, cholesky, pair_occ, hole_integrals, other_terms, occ_energy, vir_energy):
    _, rows_all, width = amplitudes.shape
    vectors = cholesky.shape[0]
    tile_n, slab_n = lax.axis_size("tile"), lax.axis_size("slab")
    rows_dev = rows_all // slab_n
    piece = min(rows_dev, width)
    chunk = next(c for c in range(8, piece + 1, 8) if piece % c == 0 and rows_dev // c <= tile_n)
    workers = rows_dev // chunk
    groups = vectors // GROUP
    f32, bf16, dma = jnp.float32, jnp.bfloat16, pltpu.SemaphoreType.DMA
    vmem = pltpu.VMEM
    anywhere = pl.BlockSpec(memory_space=pl.ANY)
    smem = pl.BlockSpec(memory_space=pltpu.SMEM)
    return pl.pallas_call(
        functools.partial(
            kernel, tile_n, slab_n, width, vectors, chunk, workers, occ_energy.shape[0] // BLOCKS
        ),
        out_shape=jax.ShapeDtypeStruct((1, rows_dev, width), f32),
        in_specs=[anywhere, anywhere, anywhere, smem, smem, smem, pl.BlockSpec(memory_space=pltpu.VMEM)],
        out_specs=pl.BlockSpec(memory_space=pltpu.VMEM),
        scratch_shapes=[
            vmem((width, rows_all), f32),
            vmem((rows_all, width), f32),
            vmem((groups, GROUP, width, rows_all), f32),
            vmem((rows_dev, width), f32),
            vmem((BLOCKS * groups, 2 * width, GROUP * LANES), bf16),
            vmem((BLOCKS * groups, 2 * width, GROUP * LANES), bf16),
            vmem((BLOCKS, 2 * LANES, 2 * LANES), bf16),
            vmem((BLOCKS, width, width), f32),
            vmem((slab_n, rows_dev // piece, piece, width), f32),
            vmem((tile_n, chunk, width), f32),
            vmem((tile_n, chunk, width), f32),
            vmem((workers, chunk, width), f32),
            vmem((BLOCKS, width), f32),
            dma((groups,)), dma, dma, dma,
            dma((workers,)), dma((tile_n,)), dma((tile_n,)), dma((workers,)),
            dma((slab_n, rows_dev // piece)), dma((slab_n, rows_dev // piece)),
        ],
        compiler_params=pltpu.CompilerParams(
            collective_id=0, has_side_effects=True, vmem_limit_bytes=56 * 2**20
        ),
        cost_estimate=pl.CostEstimate(
            flops=12 * vectors * rows_all * width * width, bytes_accessed=4 * vectors * rows_all * LANES,
            transcendentals=0,
        ),
    )(
        amplitudes.transpose(0, 2, 1), cholesky.transpose(0, 2, 1), other_terms, pair_occ.T,
        hole_integrals, occ_energy, vir_energy.reshape(1, rows_all),
    )


def solution(mesh):
    placed = (
        P("tile", None, None),
        P("slab", None, None),
        P(),
        P(),
        P("tile", "slab", None),
        P(),
        P(),
    )
    return jax.shard_map(
        local, mesh=mesh, in_specs=placed, out_specs=P("tile", "slab", None), check_vma=False
    )
```

```python
import functools

import jax
import jax.numpy as jnp
from jax import lax
from jax.experimental import pallas as pl
from jax.experimental.pallas import tpu as pltpu
from jax.sharding import PartitionSpec as P

MESH = pl.DeviceIdType.MESH
BLOCKS = 8
GROUP = 8
LANES = 128


def split(x):
    hi = x.astype(jnp.bfloat16)
    lo = (x - hi.astype(jnp.float32)).astype(jnp.bfloat16)
    return hi, lo


def widen(x):
    pad = LANES - x.shape[1]
    return jnp.concatenate([x, jnp.zeros((x.shape[0], pad), x.dtype)], axis=1) if pad else x


def turned(x):
    pad = LANES - x.shape[0]
    x = jnp.concatenate([x, jnp.zeros((pad, x.shape[1]), x.dtype)], axis=0) if pad else x
    return x.T


def kernel(
    tile_n, slab_n, width, vectors, chunk, workers, occ_block,
    amp_hbm, chol_hbm, other_hbm, pair_ref, holes_ref, occ_ref, vir_ref,
    out_ref,
    amp_t, amp, chol, other, left, right, stacks, partial, landed, gathered, products, hole, energy,
    load_sem, amp_sem, other_sem, own_sem, send1, recv1, send2, recv2, send3, recv3,
):
    t = lax.axis_index("tile")
    s = lax.axis_index("slab")
    rows_dev = other.shape[0]
    piece = min(rows_dev, width)
    per_dest = rows_dev // piece
    dests_in_block = width // piece
    groups = vectors // GROUP
    row_start = s * rows_dev

    barrier = pltpu.get_barrier_semaphore()

    @pl.loop(1, tile_n)
    def _(k):
        pl.semaphore_signal(barrier, inc=1, device_id={"tile": lax.rem(t + k, tile_n)}, device_id_type=MESH)

    @pl.loop(1, slab_n)
    def _(k):
        pl.semaphore_signal(barrier, inc=1, device_id={"slab": lax.rem(s + k, slab_n)}, device_id_type=MESH)

    amp_copy = pltpu.make_async_copy(amp_hbm.at[0], amp_t, amp_sem)
    amp_copy.start()

    def load(g):
        return pltpu.make_async_copy(chol_hbm.at[pl.ds(g * GROUP, GROUP)], chol.at[g], load_sem.at[g])

    for g in range(groups):
        load(g).start()
    other_copy = pltpu.make_async_copy(other_hbm.at[0], other, other_sem)
    other_copy.start()

    amp_copy.wait()
    amp[...] = turned(amp_t[...])[:, :width]

    def to_worker(w):
        return pltpu.make_async_remote_copy(
            src_ref=amp.at[pl.ds(pl.multiple_of(row_start + w * chunk, 8), chunk), :],
            dst_ref=gathered.at[t],
            send_sem=send1.at[w],
            recv_sem=recv1.at[t],
            device_id={"tile": w},
            device_id_type=MESH,
        )

    def own_chunk():
        return pltpu.make_async_copy(
            amp.at[pl.ds(pl.multiple_of(row_start + t * chunk, 8), chunk), :], gathered.at[t], own_sem
        )

    def exchange():
        pl.semaphore_wait(barrier, tile_n + slab_n - 2)

        @pl.loop(0, workers)
        def _(w):
            @pl.when(w != t)
            def _():
                to_worker(w).start()

        @pl.when(t < workers)
        def _():
            own_chunk().start()

    for block in range(BLOCKS):
        t_hi, t_lo = split(widen(amp[block * width : (block + 1) * width, :]))
        rows = jnp.concatenate([t_hi, t_lo], axis=1)
        zero = jnp.zeros((LANES - width, 2 * LANES), jnp.bfloat16)
        stacks[block] = jnp.concatenate([rows, zero, rows, zero], axis=0)

    def first_group(g):
        load(g).wait()
        for j in range(GROUP):
            hi, lo = split(turned(chol[g, j]))
            lanes = slice(j * LANES, (j + 1) * LANES)
            for block in range(BLOCKS):
                part = slice(block * width, (block + 1) * width)
                right[block * groups + g, :width, lanes] = hi[part]
                right[block * groups + g, width:, lanes] = lo[part]

        @pl.loop(0, BLOCKS, unroll=2)
        def _(block):
            at = block * groups + g
            vectors_here = [
                jnp.concatenate([right[at, :width, lanes], right[at, width:, lanes]], axis=1)
                for lanes in [slice(j * LANES, (j + 1) * LANES) for j in range(GROUP)]
            ]
            both = jnp.dot(
                jnp.concatenate(vectors_here, axis=0), stacks[block], preferred_element_type=jnp.float32
            )
            w_hi, w_lo = split(both[:, :LANES] + both[:, LANES:])
            for j in range(GROUP):
                lanes = slice(j * LANES, (j + 1) * LANES)
                part = slice(j * width, (j + 1) * width)
                left[at, :width, lanes] = w_hi[part]
                left[at, width:, lanes] = w_lo[part]

        pl.when(g == 0)(exchange)

    pl.loop(0, groups)(first_group)

    def irrep(p):
        return (pair_ref[0, p] // occ_block) ^ (pair_ref[1, p] // occ_block)

    def to_pair(p):
        return pltpu.make_async_remote_copy(
            src_ref=products.at[p],
            dst_ref=hole.at[t],
            send_sem=send2.at[p],
            recv_sem=recv2.at[t],
            device_id={"tile": p},
            device_id_type=MESH,
        )

    @pl.when(t < workers)
    def _():
        own_chunk().wait()

        @pl.loop(0, tile_n)
        def _(q):
            @pl.when(q != t)
            def _():
                pltpu.make_async_remote_copy(
                    src_ref=gathered.at[q], dst_ref=gathered.at[q], send_sem=send1.at[0],
                    recv_sem=recv1.at[q], device_id={"tile": q}, device_id_type=MESH,
                ).wait_recv()

        @pl.loop(0, tile_n)
        def _(p):
            mine = irrep(p)

            def add(q, total):
                factor = jnp.where(irrep(q) == mine, holes_ref[p, q], 0.0)
                return total + factor * gathered[q]

            products[p] = lax.fori_loop(0, tile_n, add, jnp.zeros((chunk, width), jnp.float32), unroll=8)

            @pl.when(p != t)
            def _():
                to_pair(p).start()

            @pl.when(p == t)
            def _():
                hole[t] = products[p]

    s_p = irrep(t)
    chips = slab_n // 2
    x_pos, core = s // 2, lax.rem(s, 2)

    def place(k):
        if dests_in_block > 1:
            block = lax.rem(s // dests_in_block + BLOCKS - 1 - k, BLOCKS)
            return block, block * dests_in_block, 0
        d, j = k // per_dest, lax.rem(k, per_dest)
        chip = lax.rem(x_pos + chips - 1 - d // 2, chips)
        flip = lax.rem(d + chips_last(d), 2)
        dest = chip * 2 + lax.rem(core + flip, 2)
        return dest * per_dest + j, dest, j

    def chips_last(d):
        return jnp.where(d // 2 == chips - 1, 1, 0)

    def to_owner(block, dest, i, j):
        return pltpu.make_async_remote_copy(
            src_ref=partial.at[block, pl.ds(i * piece, piece), :],
            dst_ref=landed.at[s, j],
            send_sem=send3.at[dest, j],
            recv_sem=recv3.at[s, j],
            device_id={"slab": dest},
            device_id_type=MESH,
        )

    @pl.loop(0, BLOCKS)
    def _(k):
        block, dest0, j = place(k)
        partner = block ^ s_p
        total = jnp.zeros((2 * width, 2 * width), jnp.float32)
        for g in range(groups):
            total += lax.dot_general(
                left[block * groups + g], right[partner * groups + g],
                (((1,), (1,)), ((), ())), preferred_element_type=jnp.float32,
            )
        half = total[:width] + total[width:]
        partial[block] = half[:, :width] + half[:, width:]
        for i in range(dests_in_block):
            @pl.when(dest0 + i != s)
            def _():
                to_owner(block, dest0 + i, i, j).start()

    for block in range(BLOCKS):
        energy[block : block + 1, :] = vir_ref[:, block * width : (block + 1) * width]
    pair_energy = occ_ref[pair_ref[0, t]] + occ_ref[pair_ref[1, t]]
    other_copy.wait()

    @pl.loop(0, workers)
    def _(w):
        @pl.when(w != t)
        def _():
            pltpu.make_async_remote_copy(
                src_ref=hole.at[w], dst_ref=hole.at[w], send_sem=send2.at[0],
                recv_sem=recv2.at[w], device_id={"tile": w}, device_id_type=MESH,
            ).wait_recv()

    for j in range(per_dest):
        start = row_start + j * piece
        block = start // width
        offset = lax.rem(start, width)
        row_i = lax.broadcasted_iota(jnp.int32, (piece, width), 0) + offset
        col_i = lax.broadcasted_iota(jnp.int32, (piece, width), 1)
        mine = energy[pl.ds(block, 1), :]
        row_energy = jnp.sum(jnp.where(row_i == col_i, mine, 0.0), axis=1, keepdims=True)
        denominator = pair_energy - row_energy - energy[pl.ds(block ^ s_p, 1), :]
        total = partial[block, pl.ds(pl.multiple_of(offset, 8), piece), :]
        for k in range(1, slab_n):
            source = lax.rem(s + k, slab_n)
            pltpu.make_async_remote_copy(
                src_ref=landed.at[source, j], dst_ref=landed.at[source, j], send_sem=send3.at[0, 0],
                recv_sem=recv3.at[source, j], device_id={"slab": source}, device_id_type=MESH,
            ).wait_recv()
            total += landed[source, j]
        count = piece // chunk
        holes = hole[j * count : (j + 1) * count].reshape(piece, width)
        out_ref[0, j * piece : (j + 1) * piece, :] = (
            other[j * piece : (j + 1) * piece, :] + total + holes
        ) / denominator

    @pl.loop(0, workers)
    def _(w):
        @pl.when(w != t)
        def _():
            to_worker(w).wait_send()

    @pl.when(t < workers)
    def _():
        @pl.loop(0, tile_n)
        def _(p):
            @pl.when(p != t)
            def _():
                to_pair(p).wait_send()

    @pl.loop(0, BLOCKS)
    def _(k):
        block, dest0, j = place(k)
        for i in range(dests_in_block):
            @pl.when(dest0 + i != s)
            def _():
                to_owner(block, dest0 + i, i, j).wait_send()


def local(amplitudes, cholesky, pair_occ, hole_integrals, other_terms, occ_energy, vir_energy):
    _, rows_all, width = amplitudes.shape
    vectors = cholesky.shape[0]
    tile_n, slab_n = lax.axis_size("tile"), lax.axis_size("slab")
    rows_dev = rows_all // slab_n
    piece = min(rows_dev, width)
    chunk = next(c for c in range(8, piece + 1, 8) if piece % c == 0 and rows_dev // c <= tile_n)
    workers = rows_dev // chunk
    groups = vectors // GROUP
    f32, bf16, dma = jnp.float32, jnp.bfloat16, pltpu.SemaphoreType.DMA
    vmem = pltpu.VMEM
    anywhere = pl.BlockSpec(memory_space=pl.ANY)
    smem = pl.BlockSpec(memory_space=pltpu.SMEM)
    return pl.pallas_call(
        functools.partial(
            kernel, tile_n, slab_n, width, vectors, chunk, workers, occ_energy.shape[0] // BLOCKS
        ),
        out_shape=jax.ShapeDtypeStruct((1, rows_dev, width), f32),
        in_specs=[anywhere, anywhere, anywhere, smem, smem, smem, pl.BlockSpec(memory_space=pltpu.VMEM)],
        out_specs=pl.BlockSpec(memory_space=pltpu.VMEM),
        scratch_shapes=[
            vmem((width, rows_all), f32),
            vmem((rows_all, width), f32),
            vmem((groups, GROUP, width, rows_all), f32),
            vmem((rows_dev, width), f32),
            vmem((BLOCKS * groups, 2 * width, GROUP * LANES), bf16),
            vmem((BLOCKS * groups, 2 * width, GROUP * LANES), bf16),
            vmem((BLOCKS, 2 * LANES, 2 * LANES), bf16),
            vmem((BLOCKS, width, width), f32),
            vmem((slab_n, rows_dev // piece, piece, width), f32),
            vmem((tile_n, chunk, width), f32),
            vmem((tile_n, chunk, width), f32),
            vmem((workers, chunk, width), f32),
            vmem((BLOCKS, width), f32),
            dma((groups,)), dma, dma, dma,
            dma((workers,)), dma((tile_n,)), dma((tile_n,)), dma((workers,)),
            dma((slab_n, rows_dev // piece)), dma((slab_n, rows_dev // piece)),
        ],
        compiler_params=pltpu.CompilerParams(
            collective_id=0, has_side_effects=True, vmem_limit_bytes=56 * 2**20
        ),
        cost_estimate=pl.CostEstimate(
            flops=12 * vectors * rows_all * width * width, bytes_accessed=4 * vectors * rows_all * LANES,
            transcendentals=0,
        ),
    )(
        amplitudes.transpose(0, 2, 1), cholesky.transpose(0, 2, 1), other_terms, pair_occ.T,
        hole_integrals, occ_energy, vir_energy.reshape(1, rows_all),
    )


def solution(mesh):
    placed = (
        P("tile", None, None),
        P("slab", None, None),
        P(),
        P(),
        P("tile", "slab", None),
        P(),
        P(),
    )
    return jax.shard_map(
        local, mesh=mesh, in_specs=placed, out_specs=P("tile", "slab", None), check_vma=False
    )
```

```python
import functools

import jax
import jax.numpy as jnp
from jax import lax
from jax.experimental import pallas as pl
from jax.experimental.pallas import tpu as pltpu
from jax.sharding import PartitionSpec as P

MESH = pl.DeviceIdType.MESH
BLOCKS = 8
GROUP = 8
LANES = 128


def split(x):
    hi = x.astype(jnp.bfloat16)
    lo = (x - hi.astype(jnp.float32)).astype(jnp.bfloat16)
    return hi, lo


def widen(x):
    pad = LANES - x.shape[1]
    return jnp.concatenate([x, jnp.zeros((x.shape[0], pad), x.dtype)], axis=1) if pad else x


def turned(x):
    pad = LANES - x.shape[0]
    x = jnp.concatenate([x, jnp.zeros((pad, x.shape[1]), x.dtype)], axis=0) if pad else x
    return x.T


def kernel(
    tile_n, slab_n, width, vectors, chunk, workers, occ_block,
    amp_hbm, chol_hbm, other_hbm, pair_ref, holes_ref, occ_ref, vir_ref,
    out_ref,
    amp_t, amp, chol, other, left, right, stacks, partial, landed, gathered, products, hole, energy,
    load_sem, amp_sem, other_sem, own_sem, send1, recv1, send2, recv2, send3, recv3,
):
    t = lax.axis_index("tile")
    s = lax.axis_index("slab")
    rows_dev = other.shape[0]
    piece = min(rows_dev, width)
    per_dest = rows_dev // piece
    dests_in_block = width // piece
    groups = vectors // GROUP
    row_start = s * rows_dev

    barrier = pltpu.get_barrier_semaphore()

    @pl.loop(1, tile_n)
    def _(k):
        pl.semaphore_signal(barrier, inc=1, device_id={"tile": lax.rem(t + k, tile_n)}, device_id_type=MESH)

    @pl.loop(1, slab_n)
    def _(k):
        pl.semaphore_signal(barrier, inc=1, device_id={"slab": lax.rem(s + k, slab_n)}, device_id_type=MESH)

    amp_copy = pltpu.make_async_copy(amp_hbm.at[0], amp_t, amp_sem)
    amp_copy.start()

    def load(g):
        return pltpu.make_async_copy(chol_hbm.at[pl.ds(g * GROUP, GROUP)], chol.at[g], load_sem.at[g])

    for g in range(groups):
        load(g).start()
    other_copy = pltpu.make_async_copy(other_hbm.at[0], other, other_sem)
    other_copy.start()

    amp_copy.wait()
    amp[...] = turned(amp_t[...])[:, :width]

    def to_worker(w):
        return pltpu.make_async_remote_copy(
            src_ref=amp.at[pl.ds(pl.multiple_of(row_start + w * chunk, 8), chunk), :],
            dst_ref=gathered.at[t],
            send_sem=send1.at[w],
            recv_sem=recv1.at[t],
            device_id={"tile": w},
            device_id_type=MESH,
        )

    def own_chunk():
        return pltpu.make_async_copy(
            amp.at[pl.ds(pl.multiple_of(row_start + t * chunk, 8), chunk), :], gathered.at[t], own_sem
        )

    def exchange():
        pl.semaphore_wait(barrier, tile_n + slab_n - 2)

        @pl.loop(0, workers)
        def _(w):
            @pl.when(w != t)
            def _():
                to_worker(w).start()

        @pl.when(t < workers)
        def _():
            own_chunk().start()

    for block in range(BLOCKS):
        t_hi, t_lo = split(widen(amp[block * width : (block + 1) * width, :]))
        rows = jnp.concatenate([t_hi, t_lo], axis=1)
        zero = jnp.zeros((LANES - width, 2 * LANES), jnp.bfloat16)
        stacks[block] = jnp.concatenate([rows, zero, rows, zero], axis=0)

    def first_group(g):
        load(g).wait()
        for j in range(GROUP):
            hi, lo = split(turned(chol[g, j]))
            lanes = slice(j * LANES, (j + 1) * LANES)
            for block in range(BLOCKS):
                part = slice(block * width, (block + 1) * width)
                right[block * groups + g, :width, lanes] = hi[part]
                right[block * groups + g, width:, lanes] = lo[part]

        @pl.loop(0, BLOCKS, unroll=4)
        def _(block):
            at = block * groups + g
            vectors_here = [
                jnp.concatenate([right[at, :width, lanes], right[at, width:, lanes]], axis=1)
                for lanes in [slice(j * LANES, (j + 1) * LANES) for j in range(GROUP)]
            ]
            both = jnp.dot(
                jnp.concatenate(vectors_here, axis=0), stacks[block], preferred_element_type=jnp.float32
            )
            w_hi, w_lo = split(both[:, :LANES] + both[:, LANES:])
            for j in range(GROUP):
                lanes = slice(j * LANES, (j + 1) * LANES)
                part = slice(j * width, (j + 1) * width)
                left[at, :width, lanes] = w_hi[part]
                left[at, width:, lanes] = w_lo[part]

        pl.when(g == 0)(exchange)

    pl.loop(0, groups)(first_group)

    def irrep(p):
        return (pair_ref[0, p] // occ_block) ^ (pair_ref[1, p] // occ_block)

    def to_pair(p):
        return pltpu.make_async_remote_copy(
            src_ref=products.at[p],
            dst_ref=hole.at[t],
            send_sem=send2.at[p],
            recv_sem=recv2.at[t],
            device_id={"tile": p},
            device_id_type=MESH,
        )

    @pl.when(t < workers)
    def _():
        own_chunk().wait()

        @pl.loop(0, tile_n)
        def _(q):
            @pl.when(q != t)
            def _():
                pltpu.make_async_remote_copy(
                    src_ref=gathered.at[q], dst_ref=gathered.at[q], send_sem=send1.at[0],
                    recv_sem=recv1.at[q], device_id={"tile": q}, device_id_type=MESH,
                ).wait_recv()

        @pl.loop(0, tile_n)
        def _(p):
            mine = irrep(p)

            def add(q, total):
                factor = jnp.where(irrep(q) == mine, holes_ref[p, q], 0.0)
                return total + factor * gathered[q]

            products[p] = lax.fori_loop(0, tile_n, add, jnp.zeros((chunk, width), jnp.float32), unroll=8)

            @pl.when(p != t)
            def _():
                to_pair(p).start()

            @pl.when(p == t)
            def _():
                hole[t] = products[p]

    s_p = irrep(t)
    chips = slab_n // 2
    x_pos, core = s // 2, lax.rem(s, 2)

    def place(k):
        if dests_in_block > 1:
            block = lax.rem(s // dests_in_block + BLOCKS - 1 - k, BLOCKS)
            return block, block * dests_in_block, 0
        d, j = k // per_dest, lax.rem(k, per_dest)
        chip = lax.rem(x_pos + chips - 1 - d // 2, chips)
        flip = lax.rem(d + chips_last(d), 2)
        dest = chip * 2 + lax.rem(core + flip, 2)
        return dest * per_dest + j, dest, j

    def chips_last(d):
        return jnp.where(d // 2 == chips - 1, 1, 0)

    def to_owner(block, dest, i, j):
        return pltpu.make_async_remote_copy(
            src_ref=partial.at[block, pl.ds(i * piece, piece), :],
            dst_ref=landed.at[s, j],
            send_sem=send3.at[dest, j],
            recv_sem=recv3.at[s, j],
            device_id={"slab": dest},
            device_id_type=MESH,
        )

    @pl.loop(0, BLOCKS // 2)
    def _(step):
        places = [place(2 * step + n) for n in range(2)]
        for block, _, _ in places:
            partner = block ^ s_p
            total = jnp.zeros((2 * width, 2 * width), jnp.float32)
            for g in range(groups):
                total += lax.dot_general(
                    left[block * groups + g], right[partner * groups + g],
                    (((1,), (1,)), ((), ())), preferred_element_type=jnp.float32,
                )
            half = total[:width] + total[width:]
            partial[block] = half[:, :width] + half[:, width:]
        for block, dest0, j in places:
            for i in range(dests_in_block):
                @pl.when(dest0 + i != s)
                def _():
                    to_owner(block, dest0 + i, i, j).start()

    for block in range(BLOCKS):
        energy[block : block + 1, :] = vir_ref[:, block * width : (block + 1) * width]
    pair_energy = occ_ref[pair_ref[0, t]] + occ_ref[pair_ref[1, t]]
    other_copy.wait()

    @pl.loop(0, workers)
    def _(w):
        @pl.when(w != t)
        def _():
            pltpu.make_async_remote_copy(
                src_ref=hole.at[w], dst_ref=hole.at[w], send_sem=send2.at[0],
                recv_sem=recv2.at[w], device_id={"tile": w}, device_id_type=MESH,
            ).wait_recv()

    for j in range(per_dest):
        start = row_start + j * piece
        block = start // width
        offset = lax.rem(start, width)
        row_i = lax.broadcasted_iota(jnp.int32, (piece, width), 0) + offset
        col_i = lax.broadcasted_iota(jnp.int32, (piece, width), 1)
        mine = energy[pl.ds(block, 1), :]
        row_energy = jnp.sum(jnp.where(row_i == col_i, mine, 0.0), axis=1, keepdims=True)
        denominator = pair_energy - row_energy - energy[pl.ds(block ^ s_p, 1), :]
        total = partial[block, pl.ds(pl.multiple_of(offset, 8), piece), :]
        for k in range(1, slab_n):
            source = lax.rem(s + k, slab_n)
            pltpu.make_async_remote_copy(
                src_ref=landed.at[source, j], dst_ref=landed.at[source, j], send_sem=send3.at[0, 0],
                recv_sem=recv3.at[source, j], device_id={"slab": source}, device_id_type=MESH,
            ).wait_recv()
            total += landed[source, j]
        count = piece // chunk
        holes = hole[j * count : (j + 1) * count].reshape(piece, width)
        out_ref[0, j * piece : (j + 1) * piece, :] = (
            other[j * piece : (j + 1) * piece, :] + total + holes
        ) / denominator

    @pl.loop(0, workers)
    def _(w):
        @pl.when(w != t)
        def _():
            to_worker(w).wait_send()

    @pl.when(t < workers)
    def _():
        @pl.loop(0, tile_n)
        def _(p):
            @pl.when(p != t)
            def _():
                to_pair(p).wait_send()

    @pl.loop(0, BLOCKS)
    def _(k):
        block, dest0, j = place(k)
        for i in range(dests_in_block):
            @pl.when(dest0 + i != s)
            def _():
                to_owner(block, dest0 + i, i, j).wait_send()


def local(amplitudes, cholesky, pair_occ, hole_integrals, other_terms, occ_energy, vir_energy):
    _, rows_all, width = amplitudes.shape
    vectors = cholesky.shape[0]
    tile_n, slab_n = lax.axis_size("tile"), lax.axis_size("slab")
    rows_dev = rows_all // slab_n
    piece = min(rows_dev, width)
    chunk = next(c for c in range(8, piece + 1, 8) if piece % c == 0 and rows_dev // c <= tile_n)
    workers = rows_dev // chunk
    groups = vectors // GROUP
    f32, bf16, dma = jnp.float32, jnp.bfloat16, pltpu.SemaphoreType.DMA
    vmem = pltpu.VMEM
    anywhere = pl.BlockSpec(memory_space=pl.ANY)
    smem = pl.BlockSpec(memory_space=pltpu.SMEM)
    return pl.pallas_call(
        functools.partial(
            kernel, tile_n, slab_n, width, vectors, chunk, workers, occ_energy.shape[0] // BLOCKS
        ),
        out_shape=jax.ShapeDtypeStruct((1, rows_dev, width), f32),
        in_specs=[anywhere, anywhere, anywhere, smem, smem, smem, pl.BlockSpec(memory_space=pltpu.VMEM)],
        out_specs=pl.BlockSpec(memory_space=pltpu.VMEM),
        scratch_shapes=[
            vmem((width, rows_all), f32),
            vmem((rows_all, width), f32),
            vmem((groups, GROUP, width, rows_all), f32),
            vmem((rows_dev, width), f32),
            vmem((BLOCKS * groups, 2 * width, GROUP * LANES), bf16),
            vmem((BLOCKS * groups, 2 * width, GROUP * LANES), bf16),
            vmem((BLOCKS, 2 * LANES, 2 * LANES), bf16),
            vmem((BLOCKS, width, width), f32),
            vmem((slab_n, rows_dev // piece, piece, width), f32),
            vmem((tile_n, chunk, width), f32),
            vmem((tile_n, chunk, width), f32),
            vmem((workers, chunk, width), f32),
            vmem((BLOCKS, width), f32),
            dma((groups,)), dma, dma, dma,
            dma((workers,)), dma((tile_n,)), dma((tile_n,)), dma((workers,)),
            dma((slab_n, rows_dev // piece)), dma((slab_n, rows_dev // piece)),
        ],
        compiler_params=pltpu.CompilerParams(
            collective_id=0, has_side_effects=True, vmem_limit_bytes=56 * 2**20
        ),
        cost_estimate=pl.CostEstimate(
            flops=12 * vectors * rows_all * width * width, bytes_accessed=4 * vectors * rows_all * LANES,
            transcendentals=0,
        ),
    )(
        amplitudes.transpose(0, 2, 1), cholesky.transpose(0, 2, 1), other_terms, pair_occ.T,
        hole_integrals, occ_energy, vir_energy.reshape(1, rows_all),
    )


def solution(mesh):
    placed = (
        P("tile", None, None),
        P("slab", None, None),
        P(),
        P(),
        P("tile", "slab", None),
        P(),
        P(),
    )
    return jax.shard_map(
        local, mesh=mesh, in_specs=placed, out_specs=P("tile", "slab", None), check_vma=False
    )
```
